32 devices in a mesh: bulk: 4 (over y, core), pair: 8 (over z, x).
Axes of the slice: x: 2, y: 2, z: 4, core: 2. Of those that a mesh axis runs over, the one named last changes fastest.
Arguments:
- spectra: float32 [1536, 2, 2048], P(('bulk', 'pair')), may hold values from -6 to 6
- pair_bin: int32 [2, 768, 48], P(None, ('bulk', 'pair')), may hold values from 0 to 127
Outputs:
- stacks: float32 [128, 1024], P(('bulk', 'pair'))
The draws below stay inside these ranges and needn't reach their ends.
All inputs are finite; a program needn't handle non-finite values.
Results may differ from the reference program's by a relative error of at most 0.008.
Values may be sent and summed in bfloat16 or wider, within the bound.
A program may use at most 128 MiB of HBM per device.

```python
import math
import jax
import jax.numpy as jnp
import numpy as np
from jax import lax

FREQS = 2048
BAND_BINS = 32
LAGS = 1024
ROUNDS = 2
STA_DEV = 48
STATIONS = 1536
BINS = 128
N_BULK = 4
N_PAIR = 8


def plant(drawn, rng, low, high):
    longest = drawn.shape.index(max(drawn.shape))
    spots = []
    for shift in (0, 1):
        where = [jax.random.randint(jax.random.fold_in(rng, axis), (), 0, length) for axis, length in enumerate(drawn.shape)]
        where[longest] = (where[longest] + shift) % drawn.shape[longest]
        spots.append(tuple(where))
    return drawn.at[spots[0]].set(low).at[spots[1]].set(high)


def steps_of(own_key, shape, shards, low, largest):
    def one(position, parts):
        steps = jax.random.uniform(jax.random.fold_in(jax.random.fold_in(own_key, 6), position), (parts,), jnp.float32, low / len(shards), largest / len(shards))
        return jnp.repeat(jnp.exp(steps), shape[position] // parts).reshape((-1,) + (1,) * (len(shape) - position - 1))

    loudness = one(*shards[0])
    for cut in shards[1:]:
        loudness = loudness * one(*cut)
    return loudness


def cumulative_ranks(count, lean):
    weights = [(1 << 20) // math.isqrt(standing ** lean) + 1 for standing in range(1, count + 1)]
    spread = 1 + sum(weights) // (1 << 30)
    return np.cumsum(np.array([max(1, weight // spread) for weight in weights]))


def ranked(own_key, extent, amount, lean):
    table = cumulative_ranks(amount, lean)
    pick = jax.random.randint(jax.random.fold_in(own_key, 1), extent, 0, int(table[amount - 1]))
    standing = jnp.searchsorted(jnp.asarray(table, jnp.int32), pick, side="right")
    return jax.random.permutation(jax.random.fold_in(own_key, 2), amount)[standing].astype(jnp.int32)


def centred(rng, shape, width, limit, pieces=(), kind=jnp.bfloat16):
    values = width * jax.random.normal(rng, shape, jnp.float32)
    if pieces:
        values = values * steps_of(rng, shape, pieces, -0.22, 0.18)
    return jnp.clip(values, -limit, limit).astype(kind)


def setup_inputs(seed: int = 0) -> dict:
    splits = jax.random.split(jax.random.key(seed), 3)
    return {
        "spectra": centred(splits[0], (STATIONS, 2, FREQS), 1.0, 6.0, ((0, 32),), jnp.float32),
        "pair_bin": plant(ranked(splits[1], (ROUNDS, STATIONS // 2, STA_DEV), BINS, 1), jax.random.fold_in(splits[1], 3), 0, BINS - 1).astype(jnp.int32),
    }


def whiten(spectra):
    station_count = spectra.shape[0]
    power = spectra[:, 0] * spectra[:, 0] + spectra[:, 1] * spectra[:, 1]
    band_power = lax.optimization_barrier(jnp.mean(power.reshape(station_count, -1, BAND_BINS), axis=2))
    scale = lax.rsqrt(band_power + 1e-06)
    scale = jnp.repeat(scale, BAND_BINS, axis=1)
    return (spectra * scale[:, None, :]).astype(jnp.bfloat16)

def lag_table(freq_count, lag_count):
    freq_index = jnp.arange(freq_count, dtype=jnp.int32)[:, None]
    lag_index = jnp.arange(lag_count, dtype=jnp.int32)[None, :] - lag_count // 2 + 2 * freq_count
    phase = freq_index * lag_index % (2 * freq_count)
    angle = phase.astype(jnp.float32) * (math.pi / freq_count)
    return jnp.concatenate([jnp.cos(angle), -jnp.sin(angle)], axis=0).astype(jnp.bfloat16)

def cross_terms(lower_rows, upper_rows):
    lower_float = lower_rows.astype(jnp.float32)
    upper_float = upper_rows.astype(jnp.float32)
    real_part = lower_float[:, None, 0] * upper_float[None, :, 0] + lower_float[:, None, 1] * upper_float[None, :, 1]
    imag_part = lower_float[:, None, 1] * upper_float[None, :, 0] - lower_float[:, None, 0] * upper_float[None, :, 1]
    joined = jnp.concatenate([real_part, imag_part], axis=-1)
    return joined.reshape(-1, joined.shape[-1]).astype(jnp.bfloat16)

def reference(spectra, pair_bin):
    whitened = whiten(spectra)
    block_count = N_BULK * N_PAIR
    half_rows = STA_DEV // 2
    blocks = whitened.reshape(block_count, STA_DEV, 2, FREQS)
    bins_flat = pair_bin.reshape(ROUNDS, block_count, half_rows * STA_DEV)
    round_bits = [N_PAIR.bit_length() - 2, 0]

    def step(carry, block):
        stack_sum, counts = carry
        for round_index in range(ROUNDS):
            round_bit = round_bits[round_index]
            partner = jnp.bitwise_xor(block, jnp.int32(1 << round_bit))
            upper_flag = jnp.bitwise_and(jnp.right_shift(block, round_bit), 1).astype(jnp.int32)
            own_block = blocks[block]
            other_block = blocks[partner]
            lower_block = jnp.where(upper_flag == 1, other_block, own_block)
            upper_block = jnp.where(upper_flag == 1, own_block, other_block)
            rows = lax.dynamic_slice_in_dim(lower_block, (upper_flag * half_rows).astype(jnp.int32), half_rows, 0)
            terms = cross_terms(rows, upper_block).astype(jnp.float32)
            bin_ids = bins_flat[round_index, block]
            stack_sum = stack_sum.at[bin_ids].add(terms)
            counts = counts.at[bin_ids].add(jnp.ones(bin_ids.shape, jnp.float32))
        return ((stack_sum, counts), None)
    start = (jnp.zeros((BINS, 2 * FREQS), jnp.float32), jnp.zeros((BINS,), jnp.float32))
    (stack_sum, counts), _ = lax.scan(step, start, jnp.arange(block_count, dtype=jnp.int32))
    table = lag_table(FREQS, LAGS).astype(jnp.float32)
    lag_sum = jnp.dot(stack_sum, table, precision=lax.Precision.HIGHEST)
    norm = lax.rsqrt(jnp.maximum(counts, 1.0)) / math.sqrt(FREQS)
    return lag_sum * norm[:, None]
```

```python
import functools
import math

import jax
import jax.numpy as jnp
import numpy as np
from jax import lax
from jax.experimental import pallas as pl
from jax.experimental.pallas import tpu as pltpu
from jax.sharding import PartitionSpec as P

FREQS = 2048
BAND_BINS = 32
LAGS = 1024
BIN_DEV = 4
GROUP = 4
LANES = 128
QUARTER = FREQS // GROUP
WIDTH = 256
CHUNKS = QUARTER // WIDTH
ROWS = GROUP * BIN_DEV
P_STEP = 48
F32 = jnp.float32
BF16 = jnp.bfloat16
MESH = pl.DeviceIdType.MESH


def lag_table():
    freq = np.arange(FREQS)[:, None]
    lag = np.arange(LAGS)[None, :] - LAGS // 2
    angle = (freq * lag % (2 * FREQS)) * (math.pi / FREQS)
    parts = [np.cos(angle), -np.sin(angle)]
    parts = [part.reshape(-1, 1, WIDTH, LAGS) for part in parts]
    return np.concatenate(parts, axis=1).reshape(-1, 2 * WIDTH, LAGS).astype(jnp.bfloat16)


def flat_bins(bin_in):
    rounds, rows, stations = bin_in.shape
    flat = rows * stations
    ids = jnp.concatenate([bin_in[rnd] for rnd in range(rounds)], axis=0)
    lane = lax.broadcasted_iota(jnp.int32, (1, flat), 1)
    row_of = lane // stations
    column = lane - row_of * stations
    spread = (lax.broadcasted_iota(jnp.int32, (stations, flat), 0) == column).astype(F32).astype(BF16)
    high, low = (ids // 16).astype(F32).astype(BF16), (ids % 16).astype(F32).astype(BF16)
    wide = 16.0 * jnp.dot(high, spread, preferred_element_type=F32)
    wide += jnp.dot(low, spread, preferred_element_type=F32)
    out = []
    for rnd in range(rounds):
        mine = lax.broadcasted_iota(jnp.int32, (rows, flat), 0) == row_of
        out.append(jnp.sum(jnp.where(mine, wide[rnd * rows : (rnd + 1) * rows], 0.0), axis=0, keepdims=True))
    return jnp.stack(out).astype(jnp.int32)


def kernel(
    n_bulk, n_pair, x_hbm, bin_hbm, table_ref, out_ref,
    x_ref, bin_in,
    own, met, lower, bins, hot, terms, total, part, share, counts, count_share, tab, lag, lag_share,
    x_send, x_recv, b_send, b_recv, s_send, s_recv, c_send, c_recv, l_send, l_recv, t_sem, in_sem, relay,
):
    stations = x_ref.shape[0]
    n_mid = n_pair // GROUP
    groups = n_bulk * n_mid
    bulk, pair = lax.axis_index("bulk"), lax.axis_index("pair")
    side = pair // (n_pair // 2)
    across = pair % 2
    member = side * 2 + across
    mid = (pair // 2) % n_mid
    group = bulk * n_mid + mid

    def device(other_group, other_member):
        other_pair = (other_member // 2) * (n_pair // 2) + (other_group % n_mid) * 2 + other_member % 2
        return (other_group // n_mid, other_pair)

    def xor_member(step):
        flip_side, flip_x = step // 2, step % 2
        s = 1 - side if flip_side else side
        x = 1 - pair % 2 if flip_x else pair % 2
        return s * 2 + x

    def ring_group(step):
        return (group + step) % groups

    def back_group(step):
        return (group + groups - step) % groups

    inputs = [
        pltpu.make_async_copy(bin_hbm, bin_in, in_sem.at[0]),
        pltpu.make_async_copy(x_hbm, x_ref, in_sem.at[1]),
    ]
    for copy in inputs:
        copy.start()
    barrier = pltpu.get_barrier_semaphore()
    bits = [1 << k for k in range(groups.bit_length() - 1)]

    def flip_group(bit):
        return device(group + bit - 2 * bit * ((group // bit) % 2), member)

    neighbours = [device(group, xor_member(step)) for step in (1, 2)] + [flip_group(bit) for bit in bits]
    for near in neighbours:
        pl.semaphore_signal(barrier, inc=1, device_id=near, device_id_type=MESH)

    quarter_table = [
        pltpu.make_async_copy(table_ref.at[member * CHUNKS + c], tab.at[c], t_sem.at[c]) for c in range(CHUNKS)
    ]
    for copy in quarter_table:
        copy.start()

    def exchange(step, c):
        to = xor_member(step)
        return pltpu.make_async_remote_copy(
            own.at[c, to], met.at[c, member], x_send.at[step, c], x_recv.at[step, c],
            device_id=device(group, to), device_id_type=MESH,
        )

    def bin_exchange(step):
        return pltpu.make_async_remote_copy(
            bins.at[member], bins.at[member], b_send.at[step], b_recv.at[step],
            device_id=device(group, xor_member(step)), device_id_type=MESH,
        )

    band = lax.broadcasted_iota(jnp.int32, (LANES, LANES), 0) // BAND_BINS
    band_t = lax.broadcasted_iota(jnp.int32, (LANES, LANES), 1) // BAND_BINS
    average = jnp.where(band == band_t, 1.0 / BAND_BINS, 0.0).astype(BF16)

    for copy in inputs:
        copy.wait()
    bins[member] = flat_bins(bin_in)

    for c in range(CHUNKS):
        for tile in range(WIDTH // LANES):
            spots = [q * QUARTER + c * WIDTH + tile * LANES for q in range(GROUP)]
            real = jnp.concatenate([x_ref[:, 0, at : at + LANES] for at in spots], axis=0)
            imag = jnp.concatenate([x_ref[:, 1, at : at + LANES] for at in spots], axis=0)
            power = real * real + imag * imag
            high = power.astype(BF16)
            low = (power - high.astype(F32)).astype(BF16)
            band_power = jnp.dot(high, average, preferred_element_type=F32)
            band_power += jnp.dot(low, average, preferred_element_type=F32)
            scale = lax.rsqrt(band_power + 1e-06)
            real, imag = (real * scale).astype(BF16), (imag * scale).astype(BF16)
            at = tile * LANES
            for q in range(GROUP):
                own[c, q, :, at : at + LANES] = real[q * stations : (q + 1) * stations]
                own[c, q, :, WIDTH + at : WIDTH + at + LANES] = imag[q * stations : (q + 1) * stations]
        if c == 0:
            pl.semaphore_wait(barrier, len(neighbours))
            pl.semaphore_signal(relay.at[0], inc=1, device_id=device(group, xor_member(1)), device_id_type=MESH)
            pl.semaphore_signal(relay.at[1], inc=1, device_id=flip_group(bits[0]), device_id_type=MESH)
            exchange(2, c).start()
            for step in (2, 1):
                bin_exchange(step).start()
            exchange(1, c).start()
            pl.semaphore_wait(relay.at[0], 1)
            bin_exchange(3).start()
            exchange(3, c).start()
        else:
            for step in (3, 2, 1):
                exchange(step, c).start()
        met[c, member] = own[c, member]

    for k in range(1, len(bits)):
        pl.semaphore_wait(relay.at[k], 1)
        if k + 1 < len(bits):
            pl.semaphore_signal(relay.at[k + 1], inc=1, device_id=flip_group(bits[k]), device_id_type=MESH)
    for step in (1, 2, 3):
        bin_exchange(step).wait()

    n_rows = groups * ROWS
    row = lax.broadcasted_iota(jnp.int32, (n_rows, LANES), 0)
    row_group, row_member = row // ROWS, (row // BIN_DEV) % GROUP
    row_pair = (row_member // 2) * (n_pair // 2) + (row_group % n_mid) * 2 + row_member % 2
    row_bin = ((row_group // n_mid) * n_pair + row_pair) * BIN_DEV + row % BIN_DEV

    meets = ((0, 2, 0), (1, 3, 0), (0, 1, 1), (2, 3, 1))
    width = P_STEP * stations
    steps = stations // P_STEP
    seen = jnp.zeros((n_rows, LANES), F32)
    for m, (lo, up, rnd) in enumerate(meets):
        half = bins.shape[-1]
        for tile in range(2 * half // LANES):
            at = tile * LANES
            ids = bins[lo if at < half else up, rnd, :, at % half : at % half + LANES]
            chosen = jnp.where(row_bin == ids, 1.0, 0.0)
            seen += chosen
            hot[m * steps + at // width, :, at % width : at % width + LANES] = chosen.astype(BF16)
    seen = jnp.sum(seen, axis=1, keepdims=True)
    counts[...] = jnp.broadcast_to(seen, (n_rows, LANES)).reshape(groups, ROWS, LANES)

    def count_copy(step):
        return pltpu.make_async_remote_copy(
            counts.at[ring_group(step)], count_share.at[step], c_send.at[step], c_recv.at[step],
            device_id=device(ring_group(step), member), device_id_type=MESH,
        )

    @pl.loop(1, groups)
    def _(step):
        count_copy(step).start()

    def stack(c, meet, lo, up):
        up_real, up_imag = met[c, up, :, :WIDTH], met[c, up, :, WIDTH:]
        sums = None
        for k in range(steps):
            for i in range(P_STEP):
                p = k * P_STEP + i
                lo_real = jnp.broadcast_to(lower[lo, p : p + 1, :WIDTH], (stations, WIDTH)).astype(BF16)
                lo_imag = jnp.broadcast_to(lower[lo, p : p + 1, WIDTH:], (stations, WIDTH)).astype(BF16)
                at = slice(p * stations, (p + 1) * stations)
                terms[at, :WIDTH] = lo_real * up_real + lo_imag * up_imag
                terms[at, WIDTH:] = lo_imag * up_real - lo_real * up_imag
            got = jnp.dot(
                hot[meet * steps + k], terms[k * width : (k + 1) * width, :], preferred_element_type=F32
            )
            sums = got if sums is None else sums + got
        return sums

    @pl.loop(0, CHUNKS)
    def _(c):
        exchange(1, c).wait_recv()
        lower[side * 2] = met[c, side * 2].astype(F32)
        total[c] = stack(c, 2 + side, side * 2, side * 2 + 1)

    def share_copy(c, step):
        return pltpu.make_async_remote_copy(
            part.at[c, ring_group(step)], share.at[c, step], s_send.at[c, step], s_recv.at[c, step],
            device_id=device(ring_group(step), member), device_id_type=MESH,
        )

    @pl.loop(0, CHUNKS)
    def _(c):
        exchange(2, c).wait_recv()

        @pl.loop(0, 3)
        def _(j):
            @pl.when(j == 1)
            def _():
                exchange(3, c).wait_recv()

            column = (across + j) % 2
            meet = jnp.where(j == 2, 3 - side, column)
            lo = jnp.where(j == 2, 2 - side * 2, column)
            up = jnp.where(j == 2, 3 - side * 2, column + 2)
            lower[lo] = met[c, lo].astype(F32)
            total[c] += stack(c, meet, lo, up)

        part[c] = total[c].astype(BF16).reshape(groups, ROWS, 2 * WIDTH)

        @pl.loop(1, groups)
        def _(step):
            share_copy(c, step).start()

    @pl.loop(1, groups)
    def _(step):
        count_copy(step).wait()

    count = counts[group]
    for step in range(1, groups):
        count += count_share[step]
    norm = lax.rsqrt(jnp.maximum(count[:, :1], 1.0)) / math.sqrt(FREQS)

    lags = None
    for c in range(CHUNKS):
        @pl.loop(1, groups)
        def _(step):
            share_copy(c, step).wait()

        stacked = part[c, group].astype(F32)
        for step in range(1, groups):
            stacked += share[c, step].astype(F32)
        quarter_table[c].wait()
        got = jnp.dot(stacked.astype(BF16), tab[c], preferred_element_type=F32)
        lags = got if lags is None else lags + got
    lags = lags * norm
    for m in range(GROUP):
        lag[m] = lags[m * BIN_DEV : (m + 1) * BIN_DEV]

    def lag_copy(step):
        to = xor_member(step)
        return pltpu.make_async_remote_copy(
            lag.at[to], lag_share.at[step], l_send.at[step], l_recv.at[step],
            device_id=device(group, to), device_id_type=MESH,
        )

    for step in (2, 3, 1):
        lag_copy(step).start()
    for step in (1, 2, 3):
        for c in range(CHUNKS):
            exchange(step, c).wait_send()
    result = lag[member]
    for step in (1, 2, 3):
        lag_copy(step).wait()
        result += lag_share[step]
    out_ref[...] = result


def body(table, n_bulk, n_pair, spectra, pair_bin):
    stations = spectra.shape[0]
    rounds = pair_bin.shape[0]
    groups = n_bulk * n_pair // GROUP
    n_rows = groups * ROWS
    half = pair_bin.shape[1] * pair_bin.shape[2]
    steps = stations // P_STEP
    dma = pltpu.SemaphoreType.DMA
    return pl.pallas_call(
        functools.partial(kernel, n_bulk, n_pair),
        out_shape=jax.ShapeDtypeStruct((BIN_DEV, LAGS), F32),
        in_specs=[
            pl.BlockSpec(memory_space=pltpu.HBM),
            pl.BlockSpec(memory_space=pltpu.HBM),
            pl.BlockSpec(memory_space=pltpu.HBM),
        ],
        out_specs=pl.BlockSpec(memory_space=pltpu.VMEM),
        scratch_shapes=[
            pltpu.VMEM(spectra.shape, F32),
            pltpu.VMEM(pair_bin.shape, jnp.int32),
            pltpu.VMEM((CHUNKS, GROUP, stations, 2 * WIDTH), BF16),
            pltpu.VMEM((CHUNKS, GROUP, stations, 2 * WIDTH), BF16),
            pltpu.VMEM((GROUP - 1, stations, 2 * WIDTH), F32),
            pltpu.VMEM((GROUP, rounds, 1, half), jnp.int32),
            pltpu.VMEM((GROUP * steps, n_rows, P_STEP * stations), BF16),
            pltpu.VMEM((stations * stations, 2 * WIDTH), BF16),
            pltpu.VMEM((CHUNKS, n_rows, 2 * WIDTH), F32),
            pltpu.VMEM((CHUNKS, groups, ROWS, 2 * WIDTH), BF16),
            pltpu.VMEM((CHUNKS, groups, ROWS, 2 * WIDTH), BF16),
            pltpu.VMEM((groups, ROWS, LANES), F32),
            pltpu.VMEM((groups, ROWS, LANES), F32),
            pltpu.VMEM((CHUNKS, 2 * WIDTH, LAGS), BF16),
            pltpu.VMEM((GROUP, BIN_DEV, LAGS), F32),
            pltpu.VMEM((GROUP, BIN_DEV, LAGS), F32),
            dma((GROUP, CHUNKS)), dma((GROUP, CHUNKS)),
            dma((GROUP,)), dma((GROUP,)),
            dma((CHUNKS, groups)), dma((CHUNKS, groups)),
            dma((groups,)), dma((groups,)),
            dma((GROUP,)), dma((GROUP,)),
            dma((CHUNKS,)),
            dma((2,)),
            pltpu.SemaphoreType.REGULAR((max(1, groups.bit_length() - 1),)),
        ],
        compiler_params=pltpu.CompilerParams(
            collective_id=0, has_side_effects=True, vmem_limit_bytes=56529919
        ),
    )(spectra, pair_bin, jnp.asarray(table))


def solution(mesh):
    return jax.shard_map(
        functools.partial(body, lag_table(), mesh.shape["bulk"], mesh.shape["pair"]),
        mesh=mesh,
        in_specs=(P(("bulk", "pair"), None, None), P(None, ("bulk", "pair"), None)),
        out_specs=P(("bulk", "pair"), None),
        check_vma=False,
    )
```

```python
import functools
import math

import jax
import jax.numpy as jnp
import numpy as np
from jax import lax
from jax.experimental import pallas as pl
from jax.experimental.pallas import tpu as pltpu
from jax.sharding import PartitionSpec as P

FREQS = 2048
BAND_BINS = 32
LAGS = 1024
BIN_DEV = 4
GROUP = 4
LANES = 128
WIDTH = 256
COLS = 2 * WIDTH
SPAN = 2 * WIDTH
CHUNKS = FREQS // SPAN
TILES = COLS // LANES
F32 = jnp.float32
BF16 = jnp.bfloat16
MESH = pl.DeviceIdType.MESH


def lag_table():
    freq = np.arange(FREQS)[:, None]
    lag = np.arange(LAGS)[None, :] - LAGS // 2
    angle = (freq * lag % (2 * FREQS)) * (math.pi / FREQS)
    parts = [np.cos(angle), -np.sin(angle)]
    parts = [part.reshape(CHUNKS, 2, WIDTH, LAGS) for part in parts]
    return np.concatenate(parts, axis=2).astype(jnp.bfloat16)


def flat_bins(bin_in):
    rounds, rows, stations = bin_in.shape
    flat = rows * stations
    ids = jnp.concatenate([bin_in[rnd] for rnd in range(rounds)], axis=0)
    lane = lax.broadcasted_iota(jnp.int32, (1, flat), 1)
    row_of = lane // stations
    column = lane - row_of * stations
    spread = (lax.broadcasted_iota(jnp.int32, (stations, flat), 0) == column).astype(F32).astype(BF16)
    high, low = (ids // 16).astype(F32).astype(BF16), (ids % 16).astype(F32).astype(BF16)
    wide = 16.0 * jnp.dot(high, spread, preferred_element_type=F32)
    wide += jnp.dot(low, spread, preferred_element_type=F32)
    out = []
    for rnd in range(rounds):
        mine = lax.broadcasted_iota(jnp.int32, (rows, flat), 0) == row_of
        out.append(jnp.sum(jnp.where(mine, wide[rnd * rows : (rnd + 1) * rows], 0.0), axis=0, keepdims=True))
    return jnp.stack(out).astype(jnp.int32)


def kernel(
    n_bulk, n_pair, x_hbm, bin_hbm, table_hbm, out_ref,
    x_ref, bin_in, own, met, lower, bins, hot, terms, total, kept, give, got, part, share,
    counts, count_got, count_part, count_share, tab,
    x_send, x_recv, b_send, b_recv, g_send, g_recv, s_send, s_recv, c_send, c_recv, t_sem, in_sem, relay,
):
    stations = x_ref.shape[0]
    n_mid = n_pair // GROUP
    spots = n_bulk // 2 * n_mid
    peers = GROUP * spots
    n_half = peers * BIN_DEV
    bulk, pair = lax.axis_index("bulk"), lax.axis_index("pair")
    core = bulk % 2
    side = pair // (n_pair // 2)
    across = pair % 2
    half = side + across - 2 * side * across
    member = side * 2 + across
    spot = bulk // 2 * n_mid + (pair // 2) % n_mid

    def place(some_spot, some_member):
        some_pair = some_member // 2 * (n_pair // 2) + some_spot % n_mid * 2 + some_member % 2
        return some_spot // n_mid * 2 + core, some_pair

    def xor_member(step):
        flip_side, flip_x = step // 2, step % 2
        s = side + flip_side - 2 * side * flip_side
        x = across + flip_x - 2 * across * flip_x
        return s * 2 + x

    def flip_spot(bit):
        return place(spot + bit - 2 * bit * (spot // bit % 2), member)

    twin = (bulk + 1 - 2 * core, pair)
    beside, beyond = place(spot, xor_member(1)), place(spot, xor_member(2))
    links = [flip_spot(1 << k) for k in range(spots.bit_length() - 1)]

    spans = [
        pltpu.make_async_copy(
            x_hbm.at[:, :, pl.ds(c * SPAN, SPAN)], x_ref.at[:, :, pl.ds(c * SPAN, SPAN)], in_sem.at[1 + c]
        )
        for c in range(CHUNKS)
    ]
    bins_in = pltpu.make_async_copy(bin_hbm, bin_in, in_sem.at[0])
    spans[0].start()
    bins_in.start()
    for copy in spans[1:]:
        copy.start()
    barrier = pltpu.get_barrier_semaphore()
    neighbours = [beyond, beside, twin] + links
    for near in neighbours:
        pl.semaphore_signal(barrier, inc=1, device_id=near, device_id_type=MESH)
    tables = [pltpu.make_async_copy(table_hbm.at[c], tab.at[c], t_sem.at[c]) for c in range(CHUNKS)]
    for copy in tables:
        copy.start()

    def exchange(step, c):
        return pltpu.make_async_remote_copy(
            own.at[c, 1 - half], met.at[c, step], x_send.at[step, c], x_recv.at[step, c],
            device_id=beyond if step == 2 else beside, device_id_type=MESH,
        )

    def bin_exchange(step):
        return pltpu.make_async_remote_copy(
            bins.at[2 - step], bins.at[4 - step], b_send.at[step], b_recv.at[step],
            device_id=beyond if step == 2 else beside, device_id_type=MESH,
        )

    band = lax.broadcasted_iota(jnp.int32, (LANES, LANES), 0) // BAND_BINS
    band_t = lax.broadcasted_iota(jnp.int32, (LANES, LANES), 1) // BAND_BINS
    average = jnp.where(band == band_t, 1.0 / BAND_BINS, 0.0).astype(BF16)

    def whiten(c):
        spans[c].wait()
        starts = [c * SPAN + at for at in range(0, SPAN, LANES)]
        real = jnp.concatenate([x_ref[:, 0, at : at + LANES] for at in starts], axis=0)
        imag = jnp.concatenate([x_ref[:, 1, at : at + LANES] for at in starts], axis=0)
        power = real * real + imag * imag
        high = power.astype(BF16)
        low = (power - high.astype(F32)).astype(BF16)
        band_power = jnp.dot(high, average, preferred_element_type=F32)
        band_power += jnp.dot(low, average, preferred_element_type=F32)
        scale = lax.rsqrt(band_power + 1e-06)
        real, imag = (real * scale).astype(BF16), (imag * scale).astype(BF16)
        for tile in range(SPAN // LANES):
            q, at = tile * LANES // WIDTH, tile * LANES % WIDTH
            rows = slice(tile * stations, (tile + 1) * stations)
            own[c, q, :, at : at + LANES] = real[rows]
            own[c, q, :, WIDTH + at : WIDTH + at + LANES] = imag[rows]

    whiten(0)
    bins_in.wait()
    bins[:2] = flat_bins(bin_in)
    pl.semaphore_wait(barrier, len(neighbours))
    pl.semaphore_signal(relay.at[0], inc=1, device_id=beside, device_id_type=MESH)
    for step in (2, 1):
        bin_exchange(step).start()
    for c in range(CHUNKS):
        if c > 0:
            whiten(c)
        for step in (2, 1):
            exchange(step, c).start()
    met[:, 0] = own[:, half]

    n_rows = 2 * n_half
    row = lax.broadcasted_iota(jnp.int32, (n_rows, LANES), 0)
    row_half, row_in = row // n_half, row % n_half
    row_peer = row_in // BIN_DEV % 2 * (peers // 2) + row_in // (2 * BIN_DEV)
    row_member, row_spot = row_peer // spots, (spot + row_peer % spots) % spots
    row_side, row_across = row_member // 2, row_member % 2
    row_side = side + row_side - 2 * side * row_side
    row_across = across + row_across - 2 * across * row_across
    row_core = core + row_half - 2 * core * row_half
    row_pair = row_side * (n_pair // 2) + row_spot % n_mid * 2 + row_across
    row_bin = ((row_spot // n_mid * 2 + row_core) * n_pair + row_pair) * BIN_DEV + row % BIN_DEV

    for k in range(len(links) + 1):
        pl.semaphore_wait(relay.at[k], 1)
        if k < len(links):
            pl.semaphore_signal(relay.at[k + 1], inc=1, device_id=links[k], device_id_type=MESH)

    seen = jnp.zeros((n_rows, LANES), F32)
    flat = bins.shape[-1]
    for rnd, is_up in ((1, across), (0, side)):
        bin_exchange(2 - rnd).wait()
        for tile in range(2 * flat // LANES):
            at = tile * LANES
            slot = rnd + 2 * is_up if at < flat else rnd + 2 - 2 * is_up
            ids = bins[slot, :, at % flat : at % flat + LANES]
            chosen = jnp.where(row_bin == ids, 1.0, 0.0)
            seen += chosen
            hot[rnd, :, at : at + LANES] = chosen.astype(BF16)
    seen = jnp.sum(seen, axis=1, keepdims=True)
    counts[...] = jnp.broadcast_to(seen, (n_rows, LANES)).reshape(2, peers // 2, 2 * BIN_DEV, LANES)

    count_swap = pltpu.make_async_remote_copy(
        counts.at[1], count_got, g_send.at[CHUNKS], g_recv.at[CHUNKS], device_id=twin, device_id_type=MESH
    )
    count_swap.start()

    def count_copy(block):
        to = place((spot + block % spots) % spots, xor_member(block // spots * 3))
        return pltpu.make_async_remote_copy(
            count_part.at[block], count_share.at[block], c_send.at[block], c_recv.at[block],
            device_id=to, device_id_type=MESH,
        )

    def stack(c, rnd, is_up):
        partner = 2 - rnd
        lo, up = partner * is_up, partner - partner * is_up
        up_real, up_imag = met[c, up, :, :WIDTH], met[c, up, :, WIDTH:]
        lower[...] = met[c, lo].astype(F32)
        for p in range(stations):
            lo_real = jnp.broadcast_to(lower[p : p + 1, :WIDTH], (stations, WIDTH)).astype(BF16)
            lo_imag = jnp.broadcast_to(lower[p : p + 1, WIDTH:], (stations, WIDTH)).astype(BF16)
            at = slice(p * stations, (p + 1) * stations)
            terms[at, :WIDTH] = lo_real * up_real + lo_imag * up_imag
            terms[at, WIDTH:] = lo_imag * up_real - lo_real * up_imag
        return jnp.dot(hot[rnd], terms[...], preferred_element_type=F32)

    @pl.loop(0, CHUNKS)
    def _(c):
        exchange(1, c).wait_recv()
        total[c] = stack(c, 1, across)

    count_swap.wait()
    count_part[...] = counts[0] + count_got[...]
    for block in range(1, 2 * spots):
        count_copy(block).start()

    def swap(c):
        return pltpu.make_async_remote_copy(
            give.at[c], got.at[c], g_send.at[c], g_recv.at[c], device_id=twin, device_id_type=MESH
        )

    def share_copy(c, peer):
        to = place((spot + peer % spots) % spots, xor_member(peer // spots))
        return pltpu.make_async_remote_copy(
            part.at[c, peer], share.at[c, peer], s_send.at[c, peer], s_recv.at[c, peer],
            device_id=to, device_id_type=MESH,
        )

    first_rows = lax.broadcasted_iota(jnp.int32, (n_half, LANES), 0) % (2 * BIN_DEV) < BIN_DEV

    def finish(c):
        swap(c).wait_recv()
        sums = kept[c] + got[c].astype(F32)
        even, odd = [], []
        for at in range(0, COLS, 2 * LANES):
            first, second = sums[:, at : at + LANES], sums[:, at + LANES : at + 2 * LANES]
            picked = jnp.where(first_rows, first, pltpu.roll(second, BIN_DEV, 0))
            even.append(picked.reshape(peers // 2, 2 * BIN_DEV, LANES))
            picked = jnp.where(first_rows, pltpu.roll(first, n_half - BIN_DEV, 0), second)
            odd.append(picked.reshape(peers // 2, 2 * BIN_DEV, LANES))
        part[c, : peers // 2] = jnp.concatenate(even, axis=1).astype(BF16)
        part[c, peers // 2 :] = jnp.concatenate(odd, axis=1).astype(BF16)

        @pl.loop(1, peers)
        def _(back):
            share_copy(c, peers - back).start()

    @pl.loop(0, CHUNKS)
    def _(c):
        exchange(2, c).wait_recv()
        sums = total[c] + stack(c, 0, side)
        kept[c] = sums[:n_half]
        give[c] = sums[n_half:].astype(BF16)
        swap(c).start()

        @pl.when(c > 0)
        def _():
            finish(c - 1)

    finish(CHUNKS - 1)

    for block in range(1, 2 * spots):
        count_copy(block).wait()
    count = jnp.zeros((BIN_DEV, LANES), F32)
    for block in range(2 * spots):
        piece = count_share[block] if block else count_part[0]
        count += piece[:BIN_DEV] if block < spots else piece[BIN_DEV:]
    norm = lax.rsqrt(jnp.maximum(count[:, :1], 1.0)) / math.sqrt(FREQS)
    for c in range(CHUNKS):
        for step in (1, 2):
            exchange(step, c).wait_send()
        swap(c).wait_send()

    lags = jnp.zeros((BIN_DEV, LAGS), F32)
    for c in range(CHUNKS):
        tables[c].wait()

        @pl.loop(1, peers)
        def _(peer):
            share_copy(c, peer).wait()

        for which, steps in ((half, (0, 3)), (1 - half, (1, 2))):
            stacked = None
            for step in steps:
                for near in range(spots):
                    peer = step * spots + near
                    piece = (share if peer else part)[c, peer].astype(F32)
                    stacked = piece if stacked is None else stacked + piece
            stacked = jnp.concatenate([stacked[at : at + BIN_DEV] for at in range(0, TILES * BIN_DEV, BIN_DEV)], axis=1)
            lags += jnp.dot(stacked.astype(BF16), tab[c, which], preferred_element_type=F32)
    out_ref[...] = lags * norm


def body(table, n_bulk, n_pair, spectra, pair_bin):
    stations = spectra.shape[0]
    spots = n_bulk * n_pair // (2 * GROUP)
    peers = GROUP * spots
    n_half = peers * BIN_DEV
    flat = pair_bin.shape[1] * pair_bin.shape[2]
    dma = pltpu.SemaphoreType.DMA
    return pl.pallas_call(
        functools.partial(kernel, n_bulk, n_pair),
        out_shape=jax.ShapeDtypeStruct((BIN_DEV, LAGS), F32),
        in_specs=[pl.BlockSpec(memory_space=pltpu.HBM)] * 3,
        out_specs=pl.BlockSpec(memory_space=pltpu.VMEM),
        scratch_shapes=[
            pltpu.VMEM(spectra.shape, F32),
            pltpu.VMEM(pair_bin.shape, jnp.int32),
            pltpu.VMEM((CHUNKS, 2, stations, COLS), BF16),
            pltpu.VMEM((CHUNKS, 3, stations, COLS), BF16),
            pltpu.VMEM((stations, COLS), F32),
            pltpu.VMEM((4, 1, flat), jnp.int32),
            pltpu.VMEM((2, 2 * n_half, 2 * flat), BF16),
            pltpu.VMEM((2 * flat, COLS), BF16),
            pltpu.VMEM((CHUNKS, 2 * n_half, COLS), F32),
            pltpu.VMEM((CHUNKS, n_half, COLS), F32),
            pltpu.VMEM((CHUNKS, n_half, COLS), BF16),
            pltpu.VMEM((CHUNKS, n_half, COLS), BF16),
            pltpu.VMEM((CHUNKS, peers, TILES * BIN_DEV, LANES), BF16),
            pltpu.VMEM((CHUNKS, peers, TILES * BIN_DEV, LANES), BF16),
            pltpu.VMEM((2, peers // 2, 2 * BIN_DEV, LANES), F32),
            pltpu.VMEM((peers // 2, 2 * BIN_DEV, LANES), F32),
            pltpu.VMEM((peers // 2, 2 * BIN_DEV, LANES), F32),
            pltpu.VMEM((peers // 2, 2 * BIN_DEV, LANES), F32),
            pltpu.VMEM((CHUNKS, 2, COLS, LAGS), BF16),
            dma((3, CHUNKS)), dma((3, CHUNKS)),
            dma((3,)), dma((3,)),
            dma((CHUNKS + 1,)), dma((CHUNKS + 1,)),
            dma((CHUNKS, peers)), dma((CHUNKS, peers)),
            dma((2 * spots,)), dma((2 * spots,)),
            dma((CHUNKS,)),
            dma((1 + CHUNKS,)),
            pltpu.SemaphoreType.REGULAR((spots.bit_length(),)),
        ],
        compiler_params=pltpu.CompilerParams(
            collective_id=0, has_side_effects=True, vmem_limit_bytes=56529919
        ),
    )(spectra, pair_bin, jnp.asarray(table))


def solution(mesh):
    return jax.shard_map(
        functools.partial(body, lag_table(), mesh.shape["bulk"], mesh.shape["pair"]),
        mesh=mesh,
        in_specs=(P(("bulk", "pair"), None, None), P(None, ("bulk", "pair"), None)),
        out_specs=P(("bulk", "pair"), None),
        check_vma=False,
    )
```

```python
import functools
import math

import jax
import jax.numpy as jnp
import numpy as np
from jax import lax
from jax.experimental import pallas as pl
from jax.experimental.pallas import tpu as pltpu
from jax.sharding import PartitionSpec as P

FREQS = 2048
BAND_BINS = 32
LAGS = 1024
BIN_DEV = 4
GROUP = 4
LANES = 128
WIDTH = 256
COLS = 2 * WIDTH
SPAN = 2 * WIDTH
CHUNKS = FREQS // SPAN
TILES = COLS // LANES
F32 = jnp.float32
BF16 = jnp.bfloat16
MESH = pl.DeviceIdType.MESH


def lag_table():
    freq = np.arange(FREQS)[:, None]
    lag = np.arange(LAGS)[None, :] - LAGS // 2
    angle = (freq * lag % (2 * FREQS)) * (math.pi / FREQS)
    parts = [np.cos(angle), -np.sin(angle)]
    parts = [part.reshape(CHUNKS, 2, WIDTH, LAGS) for part in parts]
    return np.concatenate(parts, axis=2).astype(jnp.bfloat16)


def flat_bins(bin_in):
    rounds, rows, stations = bin_in.shape
    flat = rows * stations
    ids = jnp.concatenate([bin_in[rnd] for rnd in range(rounds)], axis=0)
    lane = lax.broadcasted_iota(jnp.int32, (1, flat), 1)
    row_of = lane // stations
    column = lane - row_of * stations
    spread = (lax.broadcasted_iota(jnp.int32, (stations, flat), 0) == column).astype(F32).astype(BF16)
    high, low = (ids // 16).astype(F32).astype(BF16), (ids % 16).astype(F32).astype(BF16)
    wide = 16.0 * jnp.dot(high, spread, preferred_element_type=F32)
    wide += jnp.dot(low, spread, preferred_element_type=F32)
    out = []
    for rnd in range(rounds):
        mine = lax.broadcasted_iota(jnp.int32, (rows, flat), 0) == row_of
        out.append(jnp.sum(jnp.where(mine, wide[rnd * rows : (rnd + 1) * rows], 0.0), axis=0, keepdims=True))
    return jnp.stack(out).astype(jnp.int32)


def kernel(
    n_bulk, n_pair, x_hbm, bin_hbm, table_hbm, out_ref,
    x_ref, bin_in, own, met, lower, bins, hot, terms, total, kept, give, got, part, share,
    counts, count_got, count_part, count_share, tab,
    sent, x_recv, b_recv, g_recv, s_send, s_recv, c_recv, in_sem, relay,
):
    stations = x_ref.shape[0]
    n_mid = n_pair // GROUP
    n_y = n_bulk // 2
    spots = n_y * n_mid
    peers = GROUP * spots
    n_half = peers * BIN_DEV
    bulk, pair = lax.axis_index("bulk"), lax.axis_index("pair")
    core = bulk % 2
    side = pair // (n_pair // 2)
    across = pair % 2
    half = side + across - 2 * side * across
    member = side * 2 + across
    spot = bulk // 2 * n_mid + (pair // 2) % n_mid

    def place(some_spot, some_member):
        some_pair = some_member // 2 * (n_pair // 2) + some_spot % n_mid * 2 + some_member % 2
        return some_spot // n_mid * 2 + core, some_pair

    def xor_member(step):
        flip_side, flip_x = step // 2, step % 2
        s = side + flip_side - 2 * side * flip_side
        x = across + flip_x - 2 * across * flip_x
        return s * 2 + x

    def flip_spot(bit):
        return place(spot + bit - 2 * bit * (spot // bit % 2), member)

    twin = (bulk + 1 - 2 * core, pair)
    beside, beyond = place(spot, xor_member(1)), place(spot, xor_member(2))
    links = [flip_spot(1 << k) for k in range(spots.bit_length() - 1)]

    spans = [
        pltpu.make_async_copy(
            x_hbm.at[:, :, pl.ds(c * SPAN, SPAN)], x_ref.at[:, :, pl.ds(c * SPAN, SPAN)], in_sem.at[1 + c]
        )
        for c in range(CHUNKS)
    ]
    bins_in = pltpu.make_async_copy(bin_hbm, bin_in, in_sem.at[0])
    spans[0].start()
    bins_in.start()
    for copy in spans[1:]:
        copy.start()
    barrier = pltpu.get_barrier_semaphore()
    neighbours = [beyond, beside, twin] + links
    for near in neighbours:
        pl.semaphore_signal(barrier, inc=1, device_id=near, device_id_type=MESH)
    tables = pltpu.make_async_copy(table_hbm, tab, in_sem.at[1 + CHUNKS])
    tables.start()

    def exchange(step, c):
        return pltpu.make_async_remote_copy(
            own.at[c, 1 - half], met.at[c, step], sent.at[0], x_recv.at[step - 1, c],
            device_id=beyond if step == 2 else beside, device_id_type=MESH,
        )

    def bin_exchange(step):
        return pltpu.make_async_remote_copy(
            bins.at[2 - step], bins.at[4 - step], sent.at[1], b_recv.at[step - 1],
            device_id=beyond if step == 2 else beside, device_id_type=MESH,
        )

    band = lax.broadcasted_iota(jnp.int32, (LANES, LANES), 0) // BAND_BINS
    band_t = lax.broadcasted_iota(jnp.int32, (LANES, LANES), 1) // BAND_BINS
    average = jnp.where(band == band_t, 1.0 / BAND_BINS, 0.0).astype(BF16)

    def whiten(c):
        spans[c].wait()
        starts = [c * SPAN + at for at in range(0, SPAN, LANES)]
        real = jnp.concatenate([x_ref[:, 0, at : at + LANES] for at in starts], axis=0)
        imag = jnp.concatenate([x_ref[:, 1, at : at + LANES] for at in starts], axis=0)
        power = real * real + imag * imag
        high = power.astype(BF16)
        low = (power - high.astype(F32)).astype(BF16)
        band_power = jnp.dot(high, average, preferred_element_type=F32)
        band_power += jnp.dot(low, average, preferred_element_type=F32)
        scale = lax.rsqrt(band_power + 1e-06)
        real, imag = (real * scale).astype(BF16), (imag * scale).astype(BF16)
        for tile in range(SPAN // LANES):
            q, at = tile * LANES // WIDTH, tile * LANES % WIDTH
            rows = slice(tile * stations, (tile + 1) * stations)
            own[c, q, :, at : at + LANES] = real[rows]
            own[c, q, :, WIDTH + at : WIDTH + at + LANES] = imag[rows]

    whiten(0)
    bins_in.wait()
    bins[:2] = flat_bins(bin_in)
    pl.semaphore_wait(barrier, len(neighbours))
    pl.semaphore_signal(relay.at[0], inc=1, device_id=beside, device_id_type=MESH)
    for step in (2, 1):
        bin_exchange(step).start()
    for c in range(CHUNKS):
        if c > 0:
            whiten(c)
        for step in (2, 1):
            exchange(step, c).start()
    met[:, 0] = own[:, half]

    n_rows = 2 * n_half
    row = lax.broadcasted_iota(jnp.int32, (n_rows, LANES), 0)
    row_half, row_in = row // n_half, row % n_half
    row_peer = row_in // BIN_DEV % 2 * (peers // 2) + row_in // (2 * BIN_DEV)
    row_member, row_spot = row_peer // spots, (spot + row_peer % spots) % spots
    row_side, row_across = row_member // 2, row_member % 2
    row_side = side + row_side - 2 * side * row_side
    row_across = across + row_across - 2 * across * row_across
    row_core = core + row_half - 2 * core * row_half
    row_pair = row_side * (n_pair // 2) + row_spot % n_mid * 2 + row_across
    row_bin = ((row_spot // n_mid * 2 + row_core) * n_pair + row_pair) * BIN_DEV + row % BIN_DEV

    for k in range(len(links) + 1):
        pl.semaphore_wait(relay.at[k], 1)
        if k < len(links):
            pl.semaphore_signal(relay.at[k + 1], inc=1, device_id=links[k], device_id_type=MESH)

    seen = jnp.zeros((n_rows, LANES), F32)
    flat = bins.shape[-1]
    for rnd, is_up in ((1, across), (0, side)):
        bin_exchange(2 - rnd).wait_recv()
        for tile in range(2 * flat // LANES):
            at = tile * LANES
            slot = rnd + 2 * is_up if at < flat else rnd + 2 - 2 * is_up
            ids = bins[slot, :, at % flat : at % flat + LANES]
            chosen = jnp.where(row_bin == ids, 1.0, 0.0)
            seen += chosen
            hot[rnd, :, at : at + LANES] = chosen.astype(BF16)
    seen = jnp.sum(seen, axis=1, keepdims=True)
    counts[...] = jnp.broadcast_to(seen, (n_rows, LANES)).reshape(2, peers // 2, 2 * BIN_DEV, LANES)

    count_swap = pltpu.make_async_remote_copy(
        counts.at[1], count_got, sent.at[2], g_recv.at[CHUNKS - 1], device_id=twin, device_id_type=MESH
    )
    count_swap.start()

    def count_copy(block):
        to = place((spot + block % spots) % spots, xor_member(block // spots * 3))
        return pltpu.make_async_remote_copy(
            count_part.at[block], count_share.at[block], sent.at[3], c_recv.at[0],
            device_id=to, device_id_type=MESH,
        )

    def stack(c, rnd, is_up):
        partner = 2 - rnd
        lo, up = partner * is_up, partner - partner * is_up
        up_real, up_imag = met[c, up, :, :WIDTH], met[c, up, :, WIDTH:]
        lower[...] = met[c, lo].astype(F32)
        for p in range(stations):
            lo_real = jnp.broadcast_to(lower[p : p + 1, :WIDTH], (stations, WIDTH)).astype(BF16)
            lo_imag = jnp.broadcast_to(lower[p : p + 1, WIDTH:], (stations, WIDTH)).astype(BF16)
            at = slice(p * stations, (p + 1) * stations)
            terms[at, :WIDTH] = lo_real * up_real + lo_imag * up_imag
            terms[at, WIDTH:] = lo_imag * up_real - lo_real * up_imag
        return jnp.dot(hot[rnd], terms[...], preferred_element_type=F32)

    @pl.loop(0, CHUNKS)
    def _(c):
        exchange(1, c).wait_recv()
        total[c] = stack(c, 1, across)

    count_swap.wait()
    count_part[...] = counts[0] + count_got[...]
    for block in range(1, 2 * spots):
        count_copy(block).start()

    def swap(c):
        return pltpu.make_async_remote_copy(
            give.at[c], got.at[c], sent.at[4], g_recv.at[c], device_id=twin, device_id_type=MESH
        )

    def share_starts(c, other_core):
        for i in range(peers):
            far_side, far_mid = i // (peers // 2), i // (2 * n_y) % n_mid
            far_spot, far_across = i // 2 % n_y * n_mid + far_mid, i % 2
            flip_side = side + far_side - 2 * side * far_side
            flip_x = across + far_across - 2 * across * far_across
            peer = (flip_side * 2 + flip_x) * spots + (far_spot + spots - spot) % spots
            far_pair = far_side * (n_pair // 2) + far_mid * 2 + far_across

            def copy(at, far_core):
                return pltpu.make_async_remote_copy(
                    part.at[at, peer], share.at[at, peer], s_send.at[at], s_recv.at[at],
                    device_id=(far_spot // n_mid * 2 + far_core, far_pair), device_id_type=MESH,
                )

            @pl.when(peer > 0)
            def _():
                copy(c, core).start()

            if other_core:
                copy(c + 1, 1 - core).start()

    def share_wait(at, first):
        whole = pltpu.make_async_remote_copy(
            part.at[at, pl.ds(first, peers - first)], share.at[at, pl.ds(first, peers - first)],
            s_send.at[at], s_recv.at[at], device_id=twin, device_id_type=MESH,
        )
        whole.wait()

    first_rows = lax.broadcasted_iota(jnp.int32, (n_half, LANES), 0) % (2 * BIN_DEV) < BIN_DEV

    def pack(at, sums):
        even, odd = [], []
        for col in range(0, COLS, 2 * LANES):
            first, second = sums[:, col : col + LANES], sums[:, col + LANES : col + 2 * LANES]
            picked = jnp.where(first_rows, first, pltpu.roll(second, BIN_DEV, 0))
            even.append(picked.reshape(peers // 2, 2 * BIN_DEV, LANES))
            picked = jnp.where(first_rows, pltpu.roll(first, n_half - BIN_DEV, 0), second)
            odd.append(picked.reshape(peers // 2, 2 * BIN_DEV, LANES))
        part[at, : peers // 2] = jnp.concatenate(even, axis=1).astype(BF16)
        part[at, peers // 2 :] = jnp.concatenate(odd, axis=1).astype(BF16)

    def finish(c):
        swap(c).wait_recv()
        pack(c, kept[c] + got[c].astype(F32))
        share_starts(c, False)

    last = CHUNKS - 1

    @pl.loop(0, last)
    def _(c):
        exchange(2, c).wait_recv()
        sums = total[c] + stack(c, 0, side)
        kept[c] = sums[:n_half]
        give[c] = sums[n_half:].astype(BF16)
        swap(c).start()

        @pl.when(c > 0)
        def _():
            finish(c - 1)

    finish(last - 1)
    exchange(2, last).wait_recv()
    sums = total[last] + stack(last, 0, side)
    pack(last, sums[:n_half])
    pack(last + 1, sums[n_half:])
    share_starts(last, True)

    pltpu.make_async_remote_copy(
        bins.at[pl.ds(0, 2)], bins.at[pl.ds(2, 2)], sent.at[1], b_recv.at[0], device_id=twin, device_id_type=MESH
    ).wait_send()
    pltpu.make_async_remote_copy(
        own, own, sent.at[0], x_recv.at[0, 0], device_id=twin, device_id_type=MESH
    ).wait_send()
    pltpu.make_async_remote_copy(
        give, got, sent.at[4], g_recv.at[0], device_id=twin, device_id_type=MESH
    ).wait_send()
    rest = pl.ds(1, 2 * spots - 1)
    pltpu.make_async_remote_copy(
        count_part.at[rest], count_share.at[rest], sent.at[3], c_recv.at[0], device_id=twin, device_id_type=MESH
    ).wait()
    count = jnp.zeros((BIN_DEV, LANES), F32)
    for block in range(2 * spots):
        piece = count_share[block] if block else count_part[0]
        count += piece[:BIN_DEV] if block < spots else piece[BIN_DEV:]
    norm = lax.rsqrt(jnp.maximum(count[:, :1], 1.0)) / math.sqrt(FREQS)

    lags = jnp.zeros((BIN_DEV, LAGS), F32)
    tables.wait()
    for c in range(CHUNKS):
        share_wait(c, 1)
        if c == last:
            share_wait(c + 1, 0)
        for which, steps in ((half, (0, 3)), (1 - half, (1, 2))):
            stacked = None
            for at in (c, c + 1)[: 2 if c == last else 1]:
                for step in steps:
                    for near in range(spots):
                        peer = step * spots + near
                        piece = (share if peer or at > c else part)[at, peer].astype(F32)
                        stacked = piece if stacked is None else stacked + piece
            stacked = jnp.concatenate([stacked[at : at + BIN_DEV] for at in range(0, TILES * BIN_DEV, BIN_DEV)], axis=1)
            lags += jnp.dot(stacked.astype(BF16), tab[c, which], preferred_element_type=F32)
    out_ref[...] = lags * norm


def body(table, n_bulk, n_pair, spectra, pair_bin):
    stations = spectra.shape[0]
    spots = n_bulk * n_pair // (2 * GROUP)
    peers = GROUP * spots
    n_half = peers * BIN_DEV
    flat = pair_bin.shape[1] * pair_bin.shape[2]
    dma = pltpu.SemaphoreType.DMA
    return pl.pallas_call(
        functools.partial(kernel, n_bulk, n_pair),
        out_shape=jax.ShapeDtypeStruct((BIN_DEV, LAGS), F32),
        in_specs=[pl.BlockSpec(memory_space=pltpu.HBM)] * 3,
        out_specs=pl.BlockSpec(memory_space=pltpu.VMEM),
        scratch_shapes=[
            pltpu.VMEM(spectra.shape, F32),
            pltpu.VMEM(pair_bin.shape, jnp.int32),
            pltpu.VMEM((CHUNKS, 2, stations, COLS), BF16),
            pltpu.VMEM((CHUNKS, 3, stations, COLS), BF16),
            pltpu.VMEM((stations, COLS), F32),
            pltpu.VMEM((4, 1, flat), jnp.int32),
            pltpu.VMEM((2, 2 * n_half, 2 * flat), BF16),
            pltpu.VMEM((2 * flat, COLS), BF16),
            pltpu.VMEM((CHUNKS, 2 * n_half, COLS), F32),
            pltpu.VMEM((CHUNKS - 1, n_half, COLS), F32),
            pltpu.VMEM((CHUNKS - 1, n_half, COLS), BF16),
            pltpu.VMEM((CHUNKS - 1, n_half, COLS), BF16),
            pltpu.VMEM((CHUNKS + 1, peers, TILES * BIN_DEV, LANES), BF16),
            pltpu.VMEM((CHUNKS + 1, peers, TILES * BIN_DEV, LANES), BF16),
            pltpu.VMEM((2, peers // 2, 2 * BIN_DEV, LANES), F32),
            pltpu.VMEM((peers // 2, 2 * BIN_DEV, LANES), F32),
            pltpu.VMEM((peers // 2, 2 * BIN_DEV, LANES), F32),
            pltpu.VMEM((peers // 2, 2 * BIN_DEV, LANES), F32),
            pltpu.VMEM((CHUNKS, 2, COLS, LAGS), BF16),
            dma((5,)),
            dma((2, CHUNKS)),
            dma((2,)),
            dma((CHUNKS,)),
            dma((CHUNKS + 1,)), dma((CHUNKS + 1,)),
            dma((1,)),
            dma((2 + CHUNKS,)),
            pltpu.SemaphoreType.REGULAR((spots.bit_length(),)),
        ],
        compiler_params=pltpu.CompilerParams(
            collective_id=0, has_side_effects=True, vmem_limit_bytes=56529919
        ),
    )(spectra, pair_bin, jnp.asarray(table))


def solution(mesh):
    return jax.shard_map(
        functools.partial(body, lag_table(), mesh.shape["bulk"], mesh.shape["pair"]),
        mesh=mesh,
        in_specs=(P(("bulk", "pair"), None, None), P(None, ("bulk", "pair"), None)),
        out_specs=P(("bulk", "pair"), None),
        check_vma=False,
    )
```

```python
import functools
import math

import jax
import jax.numpy as jnp
import numpy as np
from jax import lax
from jax.experimental import pallas as pl
from jax.experimental.pallas import tpu as pltpu
from jax.sharding import PartitionSpec as P

FREQS = 2048
BAND_BINS = 32
LAGS = 1024
BIN_DEV = 4
GROUP = 4
LANES = 128
WIDTH = 256
COLS = 2 * WIDTH
SPAN = 2 * WIDTH
CHUNKS = FREQS // SPAN
TILES = COLS // LANES
F32 = jnp.float32
BF16 = jnp.bfloat16
MESH = pl.DeviceIdType.MESH


def lag_table():
    freq = np.arange(FREQS)[:, None]
    lag = np.arange(LAGS)[None, :] - LAGS // 2
    angle = (freq * lag % (2 * FREQS)) * (math.pi / FREQS)
    parts = [np.cos(angle), -np.sin(angle)]
    parts = [part.reshape(CHUNKS, 2, WIDTH, LAGS) for part in parts]
    return np.concatenate(parts, axis=2).astype(jnp.bfloat16)


def flat_bins(bin_in):
    rounds, rows, stations = bin_in.shape
    flat = rows * stations
    ids = jnp.concatenate([bin_in[rnd] for rnd in range(rounds)], axis=0)
    lane = lax.broadcasted_iota(jnp.int32, (1, flat), 1)
    row_of = lane // stations
    column = lane - row_of * stations
    spread = (lax.broadcasted_iota(jnp.int32, (stations, flat), 0) == column).astype(F32).astype(BF16)
    high, low = (ids // 16).astype(F32).astype(BF16), (ids % 16).astype(F32).astype(BF16)
    wide = 16.0 * jnp.dot(high, spread, preferred_element_type=F32)
    wide += jnp.dot(low, spread, preferred_element_type=F32)
    out = []
    for rnd in range(rounds):
        mine = lax.broadcasted_iota(jnp.int32, (rows, flat), 0) == row_of
        out.append(jnp.sum(jnp.where(mine, wide[rnd * rows : (rnd + 1) * rows], 0.0), axis=0, keepdims=True))
    return jnp.stack(out).astype(jnp.int32)


def kernel(
    n_bulk, n_pair, x_hbm, bin_hbm, table_hbm, out_ref,
    x_ref, bin_in, own, met, lower, bins, hot, terms, total, kept, give, got, part, share,
    counts, count_got, count_part, count_share, tab,
    sent, x_recv, b_recv, g_recv, s_send, s_recv, c_recv, in_sem, relay,
):
    stations = x_ref.shape[0]
    n_mid = n_pair // GROUP
    n_y = n_bulk // 2
    spots = n_y * n_mid
    peers = GROUP * spots
    n_half = peers * BIN_DEV
    bulk, pair = lax.axis_index("bulk"), lax.axis_index("pair")
    core = bulk % 2
    side = pair // (n_pair // 2)
    across = pair % 2
    half = side + across - 2 * side * across
    member = side * 2 + across
    spot = bulk // 2 * n_mid + (pair // 2) % n_mid

    def place(some_spot, some_member):
        some_pair = some_member // 2 * (n_pair // 2) + some_spot % n_mid * 2 + some_member % 2
        return some_spot // n_mid * 2 + core, some_pair

    def xor_member(step):
        flip_side, flip_x = step // 2, step % 2
        s = side + flip_side - 2 * side * flip_side
        x = across + flip_x - 2 * across * flip_x
        return s * 2 + x

    def flip_spot(bit):
        return place(spot + bit - 2 * bit * (spot // bit % 2), member)

    twin = (bulk + 1 - 2 * core, pair)
    beside, beyond = place(spot, xor_member(1)), place(spot, xor_member(2))
    links = [flip_spot(1 << k) for k in range(spots.bit_length() - 1)]

    barrier = pltpu.get_barrier_semaphore()
    neighbours = [beyond, beside, twin] + links
    for near in neighbours:
        pl.semaphore_signal(barrier, inc=1, device_id=near, device_id_type=MESH)
    spans = [
        pltpu.make_async_copy(
            x_hbm.at[:, :, pl.ds(c * SPAN, SPAN)], x_ref.at[:, :, pl.ds(c * SPAN, SPAN)], in_sem.at[1 + c]
        )
        for c in range(CHUNKS)
    ]
    bins_in = pltpu.make_async_copy(bin_hbm, bin_in, in_sem.at[0])
    spans[0].start()
    bins_in.start()
    for copy in spans[1:]:
        copy.start()
    tables = pltpu.make_async_copy(table_hbm, tab, in_sem.at[1 + CHUNKS])
    tables.start()

    def exchange(step, c):
        return pltpu.make_async_remote_copy(
            own.at[c, 1 - half], met.at[c, step], sent.at[0], x_recv.at[step - 1, c],
            device_id=beyond if step == 2 else beside, device_id_type=MESH,
        )

    def bin_exchange(step):
        return pltpu.make_async_remote_copy(
            bins.at[2 - step], bins.at[4 - step], sent.at[1], b_recv.at[step - 1],
            device_id=beyond if step == 2 else beside, device_id_type=MESH,
        )

    band = lax.broadcasted_iota(jnp.int32, (LANES, LANES), 0) // BAND_BINS
    band_t = lax.broadcasted_iota(jnp.int32, (LANES, LANES), 1) // BAND_BINS
    average = jnp.where(band == band_t, 1.0 / BAND_BINS, 0.0).astype(BF16)

    prompt = (side == 1) | ((pair // 2) % n_mid >= n_mid // 2)

    def whiten(c):
        spans[c].wait()
        starts = [c * SPAN + at for at in range(0, SPAN, LANES)]
        real = jnp.concatenate([x_ref[:, 0, at : at + LANES] for at in starts], axis=0)
        imag = jnp.concatenate([x_ref[:, 1, at : at + LANES] for at in starts], axis=0)
        power = real * real + imag * imag
        high = power.astype(BF16)
        low = (power - high.astype(F32)).astype(BF16)
        band_power = jnp.dot(high, average, preferred_element_type=F32)
        band_power += jnp.dot(low, average, preferred_element_type=F32)
        scale = lax.rsqrt(band_power + 1e-06)
        real, imag = (real * scale).astype(BF16), (imag * scale).astype(BF16)
        for tile in range(SPAN // LANES):
            q, at = tile * LANES // WIDTH, tile * LANES % WIDTH
            rows = slice(tile * stations, (tile + 1) * stations)
            own[c, q, :, at : at + LANES] = real[rows]
            own[c, q, :, WIDTH + at : WIDTH + at + LANES] = imag[rows]

    whiten(0)
    bins_in.wait()
    bins[:2] = flat_bins(bin_in)
    pl.semaphore_wait(barrier, len(neighbours))
    pl.semaphore_signal(relay.at[0], inc=1, device_id=beside, device_id_type=MESH)
    for step in (2, 1):
        bin_exchange(step).start()
    for c in range(CHUNKS):
        if c > 0:
            whiten(c)
        if c < 2:
            exchange(2, c).start()
        else:
            pl.when(prompt)(exchange(2, c).start)
        exchange(1, c).start()
    met[:, 0] = own[:, half]

    n_rows = 2 * n_half
    row = lax.broadcasted_iota(jnp.int32, (n_rows, LANES), 0)
    row_half, row_in = row // n_half, row % n_half
    row_peer = row_in // BIN_DEV % 2 * (peers // 2) + row_in // (2 * BIN_DEV)
    row_member, row_spot = row_peer // spots, (spot + row_peer % spots) % spots
    row_side, row_across = row_member // 2, row_member % 2
    row_side = side + row_side - 2 * side * row_side
    row_across = across + row_across - 2 * across * row_across
    row_core = core + row_half - 2 * core * row_half
    row_pair = row_side * (n_pair // 2) + row_spot % n_mid * 2 + row_across
    row_bin = ((row_spot // n_mid * 2 + row_core) * n_pair + row_pair) * BIN_DEV + row % BIN_DEV

    for k in range(len(links) + 1):
        pl.semaphore_wait(relay.at[k], 1)
        if k < len(links):
            pl.semaphore_signal(relay.at[k + 1], inc=1, device_id=links[k], device_id_type=MESH)

    seen = jnp.zeros((n_rows, LANES), F32)
    flat = bins.shape[-1]
    for rnd, is_up in ((1, across), (0, side)):
        bin_exchange(2 - rnd).wait_recv()
        for tile in range(2 * flat // LANES):
            at = tile * LANES
            slot = rnd + 2 * is_up if at < flat else rnd + 2 - 2 * is_up
            ids = bins[slot, :, at % flat : at % flat + LANES]
            chosen = jnp.where(row_bin == ids, 1.0, 0.0)
            seen += chosen
            hot[rnd, :, at : at + LANES] = chosen.astype(BF16)
    seen = jnp.sum(seen, axis=1, keepdims=True)
    counts[...] = jnp.broadcast_to(seen, (n_rows, LANES)).reshape(2, peers // 2, 2 * BIN_DEV, LANES)

    @pl.when(jnp.logical_not(prompt))
    def _():
        for c in range(2, CHUNKS):
            exchange(2, c).start()

    count_swap = pltpu.make_async_remote_copy(
        counts.at[1], count_got, sent.at[2], g_recv.at[CHUNKS - 1], device_id=twin, device_id_type=MESH
    )
    count_swap.start()

    def count_copy(block):
        to = place((spot + block % spots) % spots, xor_member(block // spots * 3))
        return pltpu.make_async_remote_copy(
            count_part.at[block], count_share.at[block], sent.at[3], c_recv.at[0],
            device_id=to, device_id_type=MESH,
        )

    def stack(c, rnd, is_up):
        partner = 2 - rnd
        lo, up = partner * is_up, partner - partner * is_up
        up_real, up_imag = met[c, up, :, :WIDTH], met[c, up, :, WIDTH:]
        lower[...] = met[c, lo].astype(F32)
        for p in range(stations):
            lo_real = jnp.broadcast_to(lower[p : p + 1, :WIDTH], (stations, WIDTH)).astype(BF16)
            lo_imag = jnp.broadcast_to(lower[p : p + 1, WIDTH:], (stations, WIDTH)).astype(BF16)
            at = slice(p * stations, (p + 1) * stations)
            terms[at, :WIDTH] = lo_real * up_real + lo_imag * up_imag
            terms[at, WIDTH:] = lo_imag * up_real - lo_real * up_imag
        return jnp.dot(hot[rnd], terms[...], preferred_element_type=F32)

    @pl.loop(0, CHUNKS)
    def _(c):
        exchange(1, c).wait_recv()
        total[c] = stack(c, 1, across)

    count_swap.wait()
    count_part[...] = counts[0] + count_got[...]
    for block in range(1, 2 * spots):
        count_copy(block).start()

    def swap(c):
        return pltpu.make_async_remote_copy(
            give.at[c], got.at[c], sent.at[4], g_recv.at[c], device_id=twin, device_id_type=MESH
        )

    def share_starts(c, other_core, before=None):
        for i in range(peers):
            far_side, far_mid = i // (peers // 2), i // (2 * n_y) % n_mid
            far_spot, far_across = i // 2 % n_y * n_mid + far_mid, i % 2
            flip_side = side + far_side - 2 * side * far_side
            flip_x = across + far_across - 2 * across * far_across
            peer = (flip_side * 2 + flip_x) * spots + (far_spot + spots - spot) % spots
            far_pair = far_side * (n_pair // 2) + far_mid * 2 + far_across

            def copy(at, far_core):
                return pltpu.make_async_remote_copy(
                    part.at[at, peer], share.at[at, peer], s_send.at[at], s_recv.at[at],
                    device_id=(far_spot // n_mid * 2 + far_core, far_pair), device_id_type=MESH,
                )

            @pl.when(peer > 0)
            def _():
                if before is not None:
                    copy(before, core).start()
                copy(c, core).start()

            if other_core:
                copy(c + 1, 1 - core).start()

    def share_wait(at, first):
        whole = pltpu.make_async_remote_copy(
            part.at[at, pl.ds(first, peers - first)], share.at[at, pl.ds(first, peers - first)],
            s_send.at[at], s_recv.at[at], device_id=twin, device_id_type=MESH,
        )
        whole.wait()

    first_rows = lax.broadcasted_iota(jnp.int32, (n_half, LANES), 0) % (2 * BIN_DEV) < BIN_DEV

    def pack(at, sums):
        even, odd = [], []
        for col in range(0, COLS, 2 * LANES):
            first, second = sums[:, col : col + LANES], sums[:, col + LANES : col + 2 * LANES]
            picked = jnp.where(first_rows, first, pltpu.roll(second, BIN_DEV, 0))
            even.append(picked.reshape(peers // 2, 2 * BIN_DEV, LANES))
            picked = jnp.where(first_rows, pltpu.roll(first, n_half - BIN_DEV, 0), second)
            odd.append(picked.reshape(peers // 2, 2 * BIN_DEV, LANES))
        part[at, : peers // 2] = jnp.concatenate(even, axis=1).astype(BF16)
        part[at, peers // 2 :] = jnp.concatenate(odd, axis=1).astype(BF16)

    def finish(c):
        swap(c).wait_recv()
        pack(c, kept[c] + got[c].astype(F32))
        share_starts(c, False)

    last = CHUNKS - 1

    @pl.loop(0, last)
    def _(c):
        exchange(2, c).wait_recv()
        sums = total[c] + stack(c, 0, side)
        kept[c] = sums[:n_half]
        give[c] = sums[n_half:].astype(BF16)
        swap(c).start()

        @pl.when(c > 0)
        def _():
            finish(c - 1)

    swap(last - 1).wait_recv()
    pack(last - 1, kept[last - 1] + got[last - 1].astype(F32))
    exchange(2, last).wait_recv()
    sums = total[last] + stack(last, 0, side)
    pack(last, sums[:n_half])
    pack(last + 1, sums[n_half:])
    share_starts(last, True, last - 1)

    pltpu.make_async_remote_copy(
        bins.at[pl.ds(0, 2)], bins.at[pl.ds(2, 2)], sent.at[1], b_recv.at[0], device_id=twin, device_id_type=MESH
    ).wait_send()
    pltpu.make_async_remote_copy(
        own, own, sent.at[0], x_recv.at[0, 0], device_id=twin, device_id_type=MESH
    ).wait_send()
    pltpu.make_async_remote_copy(
        give, got, sent.at[4], g_recv.at[0], device_id=twin, device_id_type=MESH
    ).wait_send()
    rest = pl.ds(1, 2 * spots - 1)
    pltpu.make_async_remote_copy(
        count_part.at[rest], count_share.at[rest], sent.at[3], c_recv.at[0], device_id=twin, device_id_type=MESH
    ).wait()
    count = jnp.zeros((BIN_DEV, LANES), F32)
    for block in range(2 * spots):
        piece = count_share[block] if block else count_part[0]
        count += piece[:BIN_DEV] if block < spots else piece[BIN_DEV:]
    norm = lax.rsqrt(jnp.maximum(count[:, :1], 1.0)) / math.sqrt(FREQS)

    lags = jnp.zeros((BIN_DEV, LAGS), F32)
    tables.wait()
    for c in range(CHUNKS):
        share_wait(c, 1)
        if c == last:
            share_wait(c + 1, 0)
        for which, steps in ((half, (0, 3)), (1 - half, (1, 2))):
            stacked = None
            for at in (c, c + 1)[: 2 if c == last else 1]:
                for step in steps:
                    for near in range(spots):
                        peer = step * spots + near
                        piece = (share if peer or at > c else part)[at, peer].astype(F32)
                        stacked = piece if stacked is None else stacked + piece
            stacked = jnp.concatenate([stacked[at : at + BIN_DEV] for at in range(0, TILES * BIN_DEV, BIN_DEV)], axis=1)
            lags += jnp.dot(stacked.astype(BF16), tab[c, which], preferred_element_type=F32)
    out_ref[...] = lags * norm


def body(table, n_bulk, n_pair, spectra, pair_bin):
    stations = spectra.shape[0]
    spots = n_bulk * n_pair // (2 * GROUP)
    peers = GROUP * spots
    n_half = peers * BIN_DEV
    flat = pair_bin.shape[1] * pair_bin.shape[2]
    dma = pltpu.SemaphoreType.DMA
    return pl.pallas_call(
        functools.partial(kernel, n_bulk, n_pair),
        out_shape=jax.ShapeDtypeStruct((BIN_DEV, LAGS), F32),
        in_specs=[pl.BlockSpec(memory_space=pltpu.HBM)] * 3,
        out_specs=pl.BlockSpec(memory_space=pltpu.VMEM),
        scratch_shapes=[
            pltpu.VMEM(spectra.shape, F32),
            pltpu.VMEM(pair_bin.shape, jnp.int32),
            pltpu.VMEM((CHUNKS, 2, stations, COLS), BF16),
            pltpu.VMEM((CHUNKS, 3, stations, COLS), BF16),
            pltpu.VMEM((stations, COLS), F32),
            pltpu.VMEM((4, 1, flat), jnp.int32),
            pltpu.VMEM((2, 2 * n_half, 2 * flat), BF16),
            pltpu.VMEM((2 * flat, COLS), BF16),
            pltpu.VMEM((CHUNKS, 2 * n_half, COLS), F32),
            pltpu.VMEM((CHUNKS - 1, n_half, COLS), F32),
            pltpu.VMEM((CHUNKS - 1, n_half, COLS), BF16),
            pltpu.VMEM((CHUNKS - 1, n_half, COLS), BF16),
            pltpu.VMEM((CHUNKS + 1, peers, TILES * BIN_DEV, LANES), BF16),
            pltpu.VMEM((CHUNKS + 1, peers, TILES * BIN_DEV, LANES), BF16),
            pltpu.VMEM((2, peers // 2, 2 * BIN_DEV, LANES), F32),
            pltpu.VMEM((peers // 2, 2 * BIN_DEV, LANES), F32),
            pltpu.VMEM((peers // 2, 2 * BIN_DEV, LANES), F32),
            pltpu.VMEM((peers // 2, 2 * BIN_DEV, LANES), F32),
            pltpu.VMEM((CHUNKS, 2, COLS, LAGS), BF16),
            dma((5,)),
            dma((2, CHUNKS)),
            dma((2,)),
            dma((CHUNKS,)),
            dma((CHUNKS + 1,)), dma((CHUNKS + 1,)),
            dma((1,)),
            dma((2 + CHUNKS,)),
            pltpu.SemaphoreType.REGULAR((spots.bit_length(),)),
        ],
        compiler_params=pltpu.CompilerParams(
            collective_id=0, has_side_effects=True, vmem_limit_bytes=56529919
        ),
    )(spectra, pair_bin, jnp.asarray(table))


def solution(mesh):
    return jax.shard_map(
        functools.partial(body, lag_table(), mesh.shape["bulk"], mesh.shape["pair"]),
        mesh=mesh,
        in_specs=(P(("bulk", "pair"), None, None), P(None, ("bulk", "pair"), None)),
        out_specs=P(("bulk", "pair"), None),
        check_vma=False,
    )
```

```python
import functools
import math

import jax
import jax.numpy as jnp
import numpy as np
from jax import lax
from jax.experimental import pallas as pl
from jax.experimental.pallas import tpu as pltpu
from jax.sharding import PartitionSpec as P

FREQS = 2048
BAND_BINS = 32
LAGS = 1024
BIN_DEV = 4
GROUP = 4
LANES = 128
WIDTH = 256
COLS = 2 * WIDTH
SPAN = 2 * WIDTH
CHUNKS = FREQS // SPAN
TILES = COLS // LANES
F32 = jnp.float32
BF16 = jnp.bfloat16
MESH = pl.DeviceIdType.MESH


def lag_table():
    freq = np.arange(FREQS)[:, None]
    lag = np.arange(LAGS)[None, :] - LAGS // 2
    angle = (freq * lag % (2 * FREQS)) * (math.pi / FREQS)
    parts = [np.cos(angle), -np.sin(angle)]
    parts = [part.reshape(CHUNKS, 2, WIDTH, LAGS) for part in parts]
    return np.concatenate(parts, axis=2).astype(jnp.bfloat16)


def flat_bins(bin_in):
    rounds, rows, stations = bin_in.shape
    flat = rows * stations
    ids = jnp.concatenate([bin_in[rnd] for rnd in range(rounds)], axis=0)
    lane = lax.broadcasted_iota(jnp.int32, (1, flat), 1)
    row_of = lane // stations
    column = lane - row_of * stations
    spread = (lax.broadcasted_iota(jnp.int32, (stations, flat), 0) == column).astype(F32).astype(BF16)
    high, low = (ids // 16).astype(F32).astype(BF16), (ids % 16).astype(F32).astype(BF16)
    wide = 16.0 * jnp.dot(high, spread, preferred_element_type=F32)
    wide += jnp.dot(low, spread, preferred_element_type=F32)
    out = []
    for rnd in range(rounds):
        mine = lax.broadcasted_iota(jnp.int32, (rows, flat), 0) == row_of
        out.append(jnp.sum(jnp.where(mine, wide[rnd * rows : (rnd + 1) * rows], 0.0), axis=0, keepdims=True))
    return jnp.stack(out).astype(jnp.int32)


def kernel(
    n_bulk, n_pair, x_hbm, bin_hbm, table_hbm, out_ref,
    x_ref, bin_in, own, met, lower, bins, hot, terms, total, kept, give, got, part, share,
    counts, count_got, count_part, count_share, tab,
    sent, x_recv, b_recv, g_recv, s_send, s_recv, c_recv, in_sem, relay,
):
    stations = x_ref.shape[0]
    n_mid = n_pair // GROUP
    n_y = n_bulk // 2
    spots = n_y * n_mid
    peers = GROUP * spots
    n_half = peers * BIN_DEV
    bulk, pair = lax.axis_index("bulk"), lax.axis_index("pair")
    core = bulk % 2
    side = pair // (n_pair // 2)
    across = pair % 2
    half = side + across - 2 * side * across
    member = side * 2 + across
    spot = bulk // 2 * n_mid + (pair // 2) % n_mid

    def place(some_spot, some_member):
        some_pair = some_member // 2 * (n_pair // 2) + some_spot % n_mid * 2 + some_member % 2
        return some_spot // n_mid * 2 + core, some_pair

    def xor_member(step):
        flip_side, flip_x = step // 2, step % 2
        s = side + flip_side - 2 * side * flip_side
        x = across + flip_x - 2 * across * flip_x
        return s * 2 + x

    def flip_spot(bit):
        return place(spot + bit - 2 * bit * (spot // bit % 2), member)

    twin = (bulk + 1 - 2 * core, pair)
    beside, beyond = place(spot, xor_member(1)), place(spot, xor_member(2))
    links = [flip_spot(1 << k) for k in range(spots.bit_length() - 1)]

    barrier = pltpu.get_barrier_semaphore()
    neighbours = [beyond, beside, twin] + links
    for near in neighbours:
        pl.semaphore_signal(barrier, inc=1, device_id=near, device_id_type=MESH)
    spans = [
        pltpu.make_async_copy(
            x_hbm.at[:, :, pl.ds(c * SPAN, SPAN)], x_ref.at[:, :, pl.ds(c * SPAN, SPAN)], in_sem.at[1 + c]
        )
        for c in range(CHUNKS)
    ]
    bins_in = pltpu.make_async_copy(bin_hbm, bin_in, in_sem.at[0])
    spans[0].start()
    bins_in.start()
    for copy in spans[1:]:
        copy.start()
    tables = pltpu.make_async_copy(table_hbm, tab, in_sem.at[1 + CHUNKS])
    tables.start()

    def exchange(step, c):
        return pltpu.make_async_remote_copy(
            own.at[c, 1 - half], met.at[c, step], sent.at[0], x_recv.at[step - 1, c],
            device_id=beyond if step == 2 else beside, device_id_type=MESH,
        )

    def bin_exchange(step):
        return pltpu.make_async_remote_copy(
            bins.at[2 - step], bins.at[4 - step], sent.at[1], b_recv.at[step - 1],
            device_id=beyond if step == 2 else beside, device_id_type=MESH,
        )

    band = lax.broadcasted_iota(jnp.int32, (LANES, LANES), 0) // BAND_BINS
    band_t = lax.broadcasted_iota(jnp.int32, (LANES, LANES), 1) // BAND_BINS
    average = jnp.where(band == band_t, 1.0 / BAND_BINS, 0.0).astype(BF16)

    prompt = (side == 1) | ((pair // 2) % n_mid >= n_mid // 2)

    def whiten(c):
        spans[c].wait()
        starts = [c * SPAN + at for at in range(0, SPAN, LANES)]
        real = jnp.concatenate([x_ref[:, 0, at : at + LANES] for at in starts], axis=0)
        imag = jnp.concatenate([x_ref[:, 1, at : at + LANES] for at in starts], axis=0)
        power = real * real + imag * imag
        high = power.astype(BF16)
        low = (power - high.astype(F32)).astype(BF16)
        band_power = jnp.dot(high, average, preferred_element_type=F32)
        band_power += jnp.dot(low, average, preferred_element_type=F32)
        scale = lax.rsqrt(band_power + 1e-06)
        real, imag = (real * scale).astype(BF16), (imag * scale).astype(BF16)
        for tile in range(SPAN // LANES):
            q, at = tile * LANES // WIDTH, tile * LANES % WIDTH
            rows = slice(tile * stations, (tile + 1) * stations)
            own[c, q, :, at : at + LANES] = real[rows]
            own[c, q, :, WIDTH + at : WIDTH + at + LANES] = imag[rows]

    whiten(0)
    bins_in.wait()
    bins[:2] = flat_bins(bin_in)
    pl.semaphore_wait(barrier, len(neighbours))
    pl.semaphore_signal(relay.at[0], inc=1, device_id=beside, device_id_type=MESH)
    for step in (2, 1):
        bin_exchange(step).start()
    for c in range(CHUNKS):
        if c > 0:
            whiten(c)
        if c < 2:
            exchange(2, c).start()
        else:
            pl.when(prompt)(exchange(2, c).start)
        exchange(1, c).start()
    met[:, 0] = own[:, half]

    n_rows = 2 * n_half
    row = lax.broadcasted_iota(jnp.int32, (n_rows, LANES), 0)
    row_half, row_in = row // n_half, row % n_half
    row_peer = row_in // BIN_DEV % 2 * (peers // 2) + row_in // (2 * BIN_DEV)
    row_member, row_spot = row_peer // spots, (spot + row_peer % spots) % spots
    row_side, row_across = row_member // 2, row_member % 2
    row_side = side + row_side - 2 * side * row_side
    row_across = across + row_across - 2 * across * row_across
    row_core = core + row_half - 2 * core * row_half
    row_pair = row_side * (n_pair // 2) + row_spot % n_mid * 2 + row_across
    row_bin = ((row_spot // n_mid * 2 + row_core) * n_pair + row_pair) * BIN_DEV + row % BIN_DEV

    for k in range(len(links) + 1):
        pl.semaphore_wait(relay.at[k], 1)
        if k < len(links):
            pl.semaphore_signal(relay.at[k + 1], inc=1, device_id=links[k], device_id_type=MESH)

    seen = jnp.zeros((n_rows, LANES), F32)
    flat = bins.shape[-1]
    for rnd, is_up in ((1, across), (0, side)):
        bin_exchange(2 - rnd).wait_recv()
        for tile in range(2 * flat // LANES):
            at = tile * LANES
            slot = rnd + 2 * is_up if at < flat else rnd + 2 - 2 * is_up
            ids = bins[slot, :, at % flat : at % flat + LANES]
            chosen = jnp.where(row_bin == ids, 1.0, 0.0)
            seen += chosen
            hot[rnd, :, at : at + LANES] = chosen.astype(BF16)
    seen = jnp.sum(seen, axis=1, keepdims=True)
    counts[...] = jnp.broadcast_to(seen, (n_rows, LANES)).reshape(2, peers // 2, 2 * BIN_DEV, LANES)

    @pl.when(jnp.logical_not(prompt))
    def _():
        for c in range(2, CHUNKS):
            exchange(2, c).start()

    count_swap = pltpu.make_async_remote_copy(
        counts.at[1], count_got, sent.at[2], g_recv.at[CHUNKS - 1], device_id=twin, device_id_type=MESH
    )
    count_swap.start()

    def count_copy(block):
        to = place((spot + block % spots) % spots, xor_member(block // spots * 3))
        return pltpu.make_async_remote_copy(
            count_part.at[block], count_share.at[block], sent.at[3], c_recv.at[0],
            device_id=to, device_id_type=MESH,
        )

    def stack(c, rnd, is_up):
        partner = 2 - rnd
        lo, up = partner * is_up, partner - partner * is_up
        up_real, up_imag = met[c, up, :, :WIDTH], met[c, up, :, WIDTH:]
        lower[...] = met[c, lo].astype(F32)
        for p in range(stations):
            lo_real = jnp.broadcast_to(lower[p : p + 1, :WIDTH], (stations, WIDTH)).astype(BF16)
            lo_imag = jnp.broadcast_to(lower[p : p + 1, WIDTH:], (stations, WIDTH)).astype(BF16)
            at = slice(p * stations, (p + 1) * stations)
            terms[at, :WIDTH] = lo_real * up_real + lo_imag * up_imag
            terms[at, WIDTH:] = lo_imag * up_real - lo_real * up_imag
        return jnp.dot(hot[rnd], terms[...], preferred_element_type=F32)

    @pl.loop(0, CHUNKS)
    def _(c):
        exchange(1, c).wait_recv()
        total[c] = stack(c, 1, across)

    count_swap.wait()
    count_part[...] = counts[0] + count_got[...]
    for block in range(1, 2 * spots):
        count_copy(block).start()

    def swap(c):
        return pltpu.make_async_remote_copy(
            give.at[c], got.at[c], sent.at[4], g_recv.at[c], device_id=twin, device_id_type=MESH
        )

    def share_starts(c, other_core, before=None):
        for i in range(peers):
            far_side, far_mid = i // (peers // 2), i // (2 * n_y) % n_mid
            far_spot, far_across = i % n_y * n_mid + far_mid, i // n_y % 2
            flip_side = side + far_side - 2 * side * far_side
            flip_x = across + far_across - 2 * across * far_across
            peer = (flip_side * 2 + flip_x) * spots + (far_spot + spots - spot) % spots
            far_pair = far_side * (n_pair // 2) + far_mid * 2 + far_across

            def copy(at, far_core):
                return pltpu.make_async_remote_copy(
                    part.at[at, peer], share.at[at, peer], s_send.at[at], s_recv.at[at],
                    device_id=(far_spot // n_mid * 2 + far_core, far_pair), device_id_type=MESH,
                )

            @pl.when(peer > 0)
            def _():
                if before is not None:
                    copy(before, core).start()
                copy(c, core).start()

            if other_core:
                copy(c + 1, 1 - core).start()

    def share_wait(at, first):
        whole = pltpu.make_async_remote_copy(
            part.at[at, pl.ds(first, peers - first)], share.at[at, pl.ds(first, peers - first)],
            s_send.at[at], s_recv.at[at], device_id=twin, device_id_type=MESH,
        )
        whole.wait()

    first_rows = lax.broadcasted_iota(jnp.int32, (n_half, LANES), 0) % (2 * BIN_DEV) < BIN_DEV

    def pack(at, sums):
        even, odd = [], []
        for col in range(0, COLS, 2 * LANES):
            first, second = sums[:, col : col + LANES], sums[:, col + LANES : col + 2 * LANES]
            picked = jnp.where(first_rows, first, pltpu.roll(second, BIN_DEV, 0))
            even.append(picked.reshape(peers // 2, 2 * BIN_DEV, LANES))
            picked = jnp.where(first_rows, pltpu.roll(first, n_half - BIN_DEV, 0), second)
            odd.append(picked.reshape(peers // 2, 2 * BIN_DEV, LANES))
        part[at, : peers // 2] = jnp.concatenate(even, axis=1).astype(BF16)
        part[at, peers // 2 :] = jnp.concatenate(odd, axis=1).astype(BF16)

    def finish(c):
        swap(c).wait_recv()
        pack(c, kept[c] + got[c].astype(F32))
        share_starts(c, False)

    last = CHUNKS - 1

    @pl.loop(0, last)
    def _(c):
        exchange(2, c).wait_recv()
        sums = total[c] + stack(c, 0, side)
        kept[c] = sums[:n_half]
        give[c] = sums[n_half:].astype(BF16)
        swap(c).start()

        @pl.when(c > 0)
        def _():
            finish(c - 1)

    swap(last - 1).wait_recv()
    pack(last - 1, kept[last - 1] + got[last - 1].astype(F32))
    exchange(2, last).wait_recv()
    sums = total[last] + stack(last, 0, side)
    pack(last, sums[:n_half])
    pack(last + 1, sums[n_half:])
    share_starts(last, True, last - 1)

    pltpu.make_async_remote_copy(
        bins.at[pl.ds(0, 2)], bins.at[pl.ds(2, 2)], sent.at[1], b_recv.at[0], device_id=twin, device_id_type=MESH
    ).wait_send()
    pltpu.make_async_remote_copy(
        own, own, sent.at[0], x_recv.at[0, 0], device_id=twin, device_id_type=MESH
    ).wait_send()
    pltpu.make_async_remote_copy(
        give, got, sent.at[4], g_recv.at[0], device_id=twin, device_id_type=MESH
    ).wait_send()
    rest = pl.ds(1, 2 * spots - 1)
    pltpu.make_async_remote_copy(
        count_part.at[rest], count_share.at[rest], sent.at[3], c_recv.at[0], device_id=twin, device_id_type=MESH
    ).wait()
    count = jnp.zeros((BIN_DEV, LANES), F32)
    for block in range(2 * spots):
        piece = count_share[block] if block else count_part[0]
        count += piece[:BIN_DEV] if block < spots else piece[BIN_DEV:]
    norm = lax.rsqrt(jnp.maximum(count[:, :1], 1.0)) / math.sqrt(FREQS)

    lags = jnp.zeros((BIN_DEV, LAGS), F32)
    tables.wait()
    for c in range(CHUNKS):
        share_wait(c, 1)
        if c == last:
            share_wait(c + 1, 0)
        for which, steps in ((half, (0, 3)), (1 - half, (1, 2))):
            stacked = None
            for at in (c, c + 1)[: 2 if c == last else 1]:
                for step in steps:
                    for near in range(spots):
                        peer = step * spots + near
                        piece = (share if peer or at > c else part)[at, peer].astype(F32)
                        stacked = piece if stacked is None else stacked + piece
            stacked = jnp.concatenate([stacked[at : at + BIN_DEV] for at in range(0, TILES * BIN_DEV, BIN_DEV)], axis=1)
            lags += jnp.dot(stacked.astype(BF16), tab[c, which], preferred_element_type=F32)
    out_ref[...] = lags * norm


def body(table, n_bulk, n_pair, spectra, pair_bin):
    stations = spectra.shape[0]
    spots = n_bulk * n_pair // (2 * GROUP)
    peers = GROUP * spots
    n_half = peers * BIN_DEV
    flat = pair_bin.shape[1] * pair_bin.shape[2]
    dma = pltpu.SemaphoreType.DMA
    return pl.pallas_call(
        functools.partial(kernel, n_bulk, n_pair),
        out_shape=jax.ShapeDtypeStruct((BIN_DEV, LAGS), F32),
        in_specs=[pl.BlockSpec(memory_space=pltpu.HBM)] * 3,
        out_specs=pl.BlockSpec(memory_space=pltpu.VMEM),
        scratch_shapes=[
            pltpu.VMEM(spectra.shape, F32),
            pltpu.VMEM(pair_bin.shape, jnp.int32),
            pltpu.VMEM((CHUNKS, 2, stations, COLS), BF16),
            pltpu.VMEM((CHUNKS, 3, stations, COLS), BF16),
            pltpu.VMEM((stations, COLS), F32),
            pltpu.VMEM((4, 1, flat), jnp.int32),
            pltpu.VMEM((2, 2 * n_half, 2 * flat), BF16),
            pltpu.VMEM((2 * flat, COLS), BF16),
            pltpu.VMEM((CHUNKS, 2 * n_half, COLS), F32),
            pltpu.VMEM((CHUNKS - 1, n_half, COLS), F32),
            pltpu.VMEM((CHUNKS - 1, n_half, COLS), BF16),
            pltpu.VMEM((CHUNKS - 1, n_half, COLS), BF16),
            pltpu.VMEM((CHUNKS + 1, peers, TILES * BIN_DEV, LANES), BF16),
            pltpu.VMEM((CHUNKS + 1, peers, TILES * BIN_DEV, LANES), BF16),
            pltpu.VMEM((2, peers // 2, 2 * BIN_DEV, LANES), F32),
            pltpu.VMEM((peers // 2, 2 * BIN_DEV, LANES), F32),
            pltpu.VMEM((peers // 2, 2 * BIN_DEV, LANES), F32),
            pltpu.VMEM((peers // 2, 2 * BIN_DEV, LANES), F32),
            pltpu.VMEM((CHUNKS, 2, COLS, LAGS), BF16),
            dma((5,)),
            dma((2, CHUNKS)),
            dma((2,)),
            dma((CHUNKS,)),
            dma((CHUNKS + 1,)), dma((CHUNKS + 1,)),
            dma((1,)),
            dma((2 + CHUNKS,)),
            pltpu.SemaphoreType.REGULAR((spots.bit_length(),)),
        ],
        compiler_params=pltpu.CompilerParams(
            collective_id=0, has_side_effects=True, vmem_limit_bytes=56529919
        ),
    )(spectra, pair_bin, jnp.asarray(table))


def solution(mesh):
    return jax.shard_map(
        functools.partial(body, lag_table(), mesh.shape["bulk"], mesh.shape["pair"]),
        mesh=mesh,
        in_specs=(P(("bulk", "pair"), None, None), P(None, ("bulk", "pair"), None)),
        out_specs=P(("bulk", "pair"), None),
        check_vma=False,
    )
```
